32 devices in a mesh: frames: 16 (over z, y, core), heads: 2 (over x).
Axes of the slice: x: 2, y: 2, z: 4, core: 2. Of those that a mesh axis runs over, the one named last changes fastest.
Arguments:
- frames_x: bfloat16 [16, 4, 80, 2240], P('frames', 'heads'), may hold values from -6 to 6
- qkv_weight: bfloat16 [3, 896, 4480], P(None, 'heads'), may hold values from -0.125 to 0.125
- out_weight: bfloat16 [1792, 2240], P('heads', 'frames'), may hold values from -0.125 to 0.125
Outputs:
- attn_out: bfloat16 [16, 4, 80, 2240], P('frames', 'heads')
The draws below stay inside these ranges and needn't reach their ends.
All inputs are finite; a program needn't handle non-finite values.
Results may differ from the reference program's by a relative error of at most 0.005.
Values may be sent and summed in bfloat16 or wider, within the bound.
A program may use at most 128 MiB of HBM per device.

```python
import jax
import jax.numpy as jnp
from jax import lax

D = 2240
HEADS = 16
HD = 112
COLS = 80
ROWS = 4
FRAMES = 16


def draw_frames_x(key, part):
    first, second = jax.random.split(key, 2)
    common = jax.random.normal(first, (FRAMES, 1, 1, D), jnp.float32)
    noise = jax.random.normal(second, (FRAMES, ROWS, COLS, D), jnp.float32)
    mixed = 1.2 * common + 0.8 * noise
    return jnp.clip(mixed, -6.0, 6.0).astype(jnp.bfloat16)


def block_levels(stream_key, extent, cuts, low, high):
    def one(dim, shards_of):
        heights = jax.random.uniform(jax.random.fold_in(jax.random.fold_in(stream_key, 6), dim), (shards_of,), jnp.float32, low / len(cuts), high / len(cuts))
        return jnp.repeat(jnp.exp(heights), extent[dim] // shards_of).reshape((-1,) + (1,) * (len(extent) - dim - 1))

    loudness = one(*cuts[0])
    for cut in cuts[1:]:
        loudness = loudness * one(*cut)
    return loudness


def normal_values(key, dims, width, most, shards=(), held_as=jnp.bfloat16):
    level = block_levels(key, dims, shards, -0.22, 0.18) if shards else 1.0
    array = jax.random.normal(key, dims, jnp.float32) * width * level
    return jnp.minimum(jnp.maximum(array, -most), most).astype(held_as)


def setup_inputs(seed: int = 0) -> dict:
    key_of = jax.random.split(jax.random.key(seed), 4)
    frames_x = draw_frames_x(jax.random.fold_in(key_of[3], 71), 0)
    qkv_weight = normal_values(key_of[1], (3, HEADS * HD // 2, 2 * D), D ** -0.5, 0.125, ((1, 2),))
    out_weight = normal_values(key_of[2], (HEADS * HD, D), (HEADS * HD) ** -0.5, 0.125, ((0, 2), (1, 16)))
    return {"frames_x": frames_x, "qkv_weight": qkv_weight, "out_weight": out_weight}


EPSILON = 1e-6


def reference(frames_x, qkv_weight, out_weight):
    tokens = ROWS * COLS
    highest = lax.Precision.HIGHEST
    weights = qkv_weight.reshape(3, HEADS * HD, D)

    def one_frame(carry, frame):
        prior_state, prior_total = carry
        flat = frame.reshape(tokens, D)
        query = jax.nn.relu(jnp.dot(flat, weights[0].T, preferred_element_type=jnp.float32)).astype(jnp.bfloat16)
        keys = jax.nn.relu(jnp.dot(flat, weights[1].T, preferred_element_type=jnp.float32)).astype(jnp.bfloat16)
        values = jnp.dot(flat, weights[2].T, preferred_element_type=jnp.float32).astype(jnp.bfloat16)
        query_f = query.astype(jnp.float32).reshape(tokens, HEADS, HD)
        keys_f = keys.astype(jnp.float32).reshape(tokens, HEADS, HD)
        values_f = values.astype(jnp.float32).reshape(tokens, HEADS, HD)
        state = jnp.einsum("mhi,mhj->hij", keys_f, values_f, precision=highest)
        total = jnp.sum(keys_f, axis=0)
        cumul = prior_state + state
        cumtot = prior_total + total
        numerator = jnp.einsum("mhi,hij->mhj", query_f, cumul, precision=highest)
        denominator = jnp.einsum("mhi,hi->mh", query_f, cumtot, precision=highest) + EPSILON
        attended = (numerator / denominator[..., None]).astype(jnp.bfloat16).reshape(tokens, HEADS * HD)
        result = jnp.dot(attended, out_weight, preferred_element_type=jnp.float32).astype(jnp.bfloat16)
        return (cumul, cumtot), result.reshape(ROWS, COLS, D)

    start = (jnp.zeros((HEADS, HD, HD), jnp.float32), jnp.zeros((HEADS, HD), jnp.float32))
    finish, outputs = lax.scan(one_frame, start, frames_x)
    return outputs
```

```python
import functools

import jax
import jax.numpy as jnp
from jax import lax
from jax.experimental import pallas as pl
from jax.experimental.pallas import tpu as pltpu
from jax.sharding import PartitionSpec as P

HD = 112


EPSILON = 1e-06


def carried_in(part, axis, combine, identity):
    place = lax.axis_index(axis)
    gathered = jax.tree.map(lambda a: lax.all_gather(a, axis), part)
    state = jax.tree.map(lambda a, e: jnp.zeros_like(a) + jnp.asarray(e, a.dtype), part, identity)

    def one(turn, state):
        return combine(
            state, jax.tree.map(lambda a: lax.dynamic_index_in_dim(a, turn, 0, False), gathered)
        )

    return lax.fori_loop(0, place, one, state)


def add_states(earlier, later):
    return (earlier[0] + later[0], earlier[1] + later[1])


def on_device(frames_x, qkv_weight, out_weight):
    feature_count = qkv_weight.shape[2] // 2
    local_width = qkv_weight.shape[1] * 2
    head_count = local_width // HD
    highest = lax.Precision.HIGHEST
    weights = qkv_weight.reshape(3, local_width, feature_count)
    mixed = jnp.einsum(
        "frcd,sed->sfrce",
        lax.all_gather(frames_x, "heads", axis=1, tiled=True),
        weights,
        preferred_element_type=jnp.float32,
    )
    projected = jnp.stack([jax.nn.relu(mixed[0]), jax.nn.relu(mixed[1]), mixed[2]]).astype(
        jnp.bfloat16
    )
    frame_count, row_count, col_count = (projected.shape[1], projected.shape[2], projected.shape[3])
    tokens = frame_count * row_count * col_count
    query = projected[0].reshape(tokens, head_count, HD)
    keys = projected[1].reshape(tokens, head_count, HD)
    values = projected[2].reshape(tokens, head_count, HD)
    own_state = jnp.einsum("mhi,mhj->hij", keys, values, preferred_element_type=jnp.float32)
    own_total = jnp.sum(keys.astype(jnp.float32), axis=0)
    identity = (jnp.zeros_like(own_state), jnp.zeros_like(own_total))
    prior_state, prior_total = carried_in((own_state, own_total), "frames", add_states, identity)
    query_wide = query.astype(jnp.float32)
    numerator = jnp.einsum("mhi,hij->mhj", query_wide, prior_state + own_state, precision=highest)
    denominator = (
        jnp.einsum("mhi,hi->mh", query_wide, prior_total + own_total, precision=highest) + EPSILON
    )
    attended = (numerator / denominator[..., None]).astype(jnp.bfloat16)
    attended = attended.reshape(frame_count, row_count, col_count, local_width)
    by_rows = lax.all_to_all(attended, "heads", split_axis=1, concat_axis=3, tiled=True)
    full_rows = lax.all_gather(out_weight, "heads", axis=0, tiled=True)
    result = jnp.einsum(
        "frce,ed->frcd",
        by_rows,
        lax.all_gather(full_rows, "frames", axis=1, tiled=True),
        preferred_element_type=jnp.float32,
    )
    return result.astype(jnp.bfloat16)


MESH = pl.DeviceIdType.MESH
NT = (((1,), (1,)), ((), ()))
TN = (((0,), (0,)), ((), ()))
F32 = jnp.float32
BF16 = jnp.bfloat16
PLANES = 4


def dot(a, b, dims):
    return lax.dot_general(a, b, dims, preferred_element_type=F32)


def kernel(
    x_ref, w_ref, wo_ref, out_ref,
    xv, xp, xe, xo, wv, wov, wog, qs, ks, vs, st, stb, cst, yb, yst, zb, zst, pb, pst, cum,
    att, po, pin, acc,
    lsem, x_send, x_recv, w_send, w_recv, s_send, s_recv, p_send, p_recv,
):
    frame = lax.axis_index("frames")
    side = lax.axis_index("heads")
    core = frame % 2
    y = (frame // 2) % 2
    z = frame // 4
    rows, d = x_ref.shape
    half_rows = w_ref.shape[1]
    width = wo_ref.shape[0]
    cols = wo_ref.shape[1]
    block = wog.shape[1]
    wide = xe.shape[1]
    heads = width // HD
    sub = HD // 2
    pad = wide - d
    lanes = st.shape[1] // 2

    x_peer = (frame, 1 - side)
    core_peer = (frame + 1 - 2 * core, side)
    y_peer = (frame + 2 - 4 * y, side)

    def z_peer(step):
        return ((frame + 4 * step) % (4 * PLANES), side)

    peers = [x_peer, core_peer, y_peer] + [z_peer(k) for k in range(1, PLANES)]

    load_wo = pltpu.make_async_copy(wo_ref, wov, lsem.at[0])
    load_x = pltpu.make_async_copy(x_ref, xv, lsem.at[1])
    load_w = [pltpu.make_async_copy(w_ref.at[s], wv.at[s], lsem.at[2 + s]) for s in range(3)]

    barrier = pltpu.get_barrier_semaphore()
    for peer in peers:
        pl.semaphore_signal(barrier, inc=1, device_id=peer, device_id_type=MESH)
    load_wo.start()
    load_x.start()
    for s in (1, 2, 0):
        load_w[s].start()
    pl.semaphore_wait(barrier, len(peers))

    def remote(src, dst, send, recv, peer):
        return pltpu.make_async_remote_copy(
            src_ref=src, dst_ref=dst, send_sem=send, recv_sem=recv,
            device_id=peer, device_id_type=MESH,
        )

    parts = xp.shape[0] // CHUNK
    x_copies = []
    for k in range(parts):
        span = pl.ds(k * CHUNK, CHUNK)
        c = remote(x_ref.at[span], xp.at[span], x_send.at[k], x_recv.at[k], x_peer)
        c.start()
        x_copies.append(c)

    load_wo.wait()
    row = lax.broadcasted_iota(jnp.int32, (width, width), 0)
    col = lax.broadcasted_iota(jnp.int32, (width, width), 1)
    target = jnp.where(col < half_rows, 2 * col, 2 * (col - half_rows) + 1)
    order = jnp.where(row == target, 1.0, 0.0).astype(BF16)
    wog[frame, pl.ds(0, cols), :] = dot(wov[...], order, TN).astype(BF16)

    wog[frame, pl.ds(cols, block - cols), :] = jnp.zeros((block - cols, width), BF16)
    w_copies = []

    def send_block(which, peer, slot):
        c = remote(wog.at[which], wog.at[which], w_send.at[slot], w_recv.at[which], peer)
        c.start()
        w_copies.append(c)

    def wait_block(which):
        remote(wog.at[which], wog.at[which], w_send.at[0], w_recv.at[which], core_peer).wait_recv()

    for k in range(1, PLANES):
        send_block(frame, z_peer(k), k - 1)
    send_block(frame, y_peer, 3)
    send_block(frame, core_peer, 4)

    def place(src, at, count, start):
        xe[start : start + count, 0:d] = src[at : at + count, :]
        xe[start : start + count, d:wide] = jnp.zeros((count, pad), BF16)
        xo[start : start + count, pad:wide] = src[at : at + count, :]
        xo[start : start + count, 0:pad] = jnp.zeros((count, pad), BF16)

    def project(s, dst, start, count, relu):
        for j, (src, lo) in enumerate(((xe, 0), (xo, d - pad))):
            p = dot(src[start : start + count, :], wv[s, :, lo : lo + wide], NT)
            if relu:
                p = jnp.maximum(p, 0.0)
            dst[start : start + count, j * lanes : j * lanes + half_rows] = p.astype(BF16)

    total = qs.shape[0]
    vs[:, half_rows:lanes] = jnp.ones((total, lanes - half_rows), BF16)
    vs[:, lanes + half_rows : 2 * lanes] = jnp.zeros((total, lanes - half_rows), BF16)

    load_x.wait()
    place(xv, 0, rows, 0)
    load_w[1].wait()
    project(1, ks, 0, rows, True)
    load_w[2].wait()
    project(2, vs, 0, rows, False)

    y_own = 4 * z + 2 * (1 - y) + core

    def forward_z(k):
        which = (frame + 4 * (PLANES - k)) % (4 * PLANES)
        wait_block(which)
        send_block(which, y_peer, 5 + 2 * k)
        send_block(which, core_peer, 6 + 2 * k)

    wait_block(y_own)
    send_block(y_own, core_peer, 5)

    load_w[0].wait()
    project(0, qs, 0, rows, True)

    for k in range(parts):
        x_copies[k].wait_recv()
        place(xp, k * CHUNK, CHUNK, rows + k * CHUNK)
        project(1, ks, rows + k * CHUNK, CHUNK, True)
        project(2, vs, rows + k * CHUNK, CHUNK, False)

    srow = lax.broadcasted_iota(jnp.int32, (half_rows, lanes), 0) // sub
    scol = lax.broadcasted_iota(jnp.int32, (half_rows, lanes), 1)
    mask = srow == jnp.where(scol < half_rows, scol // sub, scol - half_rows)

    for i in range(2):
        for j in range(2):
            full = dot(
                ks[:, i * lanes : i * lanes + half_rows],
                vs[:, j * lanes : (j + 1) * lanes],
                TN,
            )
            full = jnp.where(mask, full, 0.0)
            small = full[0:sub]
            for h in range(1, heads):
                small = small + full[h * sub : (h + 1) * sub]
            st[i * sub : (i + 1) * sub, j * lanes : (j + 1) * lanes] = small
    stb[...] = st[...].astype(BF16)
    c_core = remote(stb, cst, s_send.at[0], s_recv.at[0], core_peer)
    c_core.start()
    c_core.wait_recv()

    mine = pl.ds(pl.multiple_of(core * lanes, 128), lanes)
    other = pl.ds(pl.multiple_of((1 - core) * lanes, 128), lanes)
    pair = st[:, mine] + cst[:, mine].astype(F32)
    yb[...] = pair.astype(BF16)
    c_y = remote(yb, yst, s_send.at[1], s_recv.at[1], y_peer)
    c_y.start()
    c_y.wait_recv()
    zb[...] = (pair + yst[...].astype(F32)).astype(BF16)

    for k in range(1, PLANES):
        @pl.when(z + k < PLANES)
        def _():
            remote(zb, zst.at[k - 1], s_send.at[1 + k], s_recv.at[1 + k], z_peer(k)).start()

    for k in range(1, PLANES):
        forward_z(k)

    project(0, qs, rows, rows, True)

    cum[...] = st[...] + cst[...].astype(F32) * core.astype(F32)
    prior = yst[...].astype(F32) * y.astype(F32)
    pb[...] = prior.astype(BF16)
    acc[0:HD, 0:lanes] = prior
    for k in range(1, PLANES):
        @pl.when(z >= k)
        def _():
            remote(zb, zst.at[k - 1], s_send.at[1 + k], s_recv.at[1 + k], z_peer(k)).wait_recv()
            acc[0:HD, 0:lanes] += zst[k - 1].astype(F32)
    pb[...] = acc[0:HD, 0:lanes].astype(BF16)
    c_p = remote(pb, pst, s_send.at[1 + PLANES], s_recv.at[1 + PLANES], core_peer)
    c_p.start()
    cum[:, mine] += acc[0:HD, 0:lanes]
    c_p.wait_recv()
    cum[:, other] += pst[...].astype(F32)

    nums = []
    for j in range(2):
        num = None
        for i in range(2):
            part = cum[i * sub : (i + 1) * sub, j * lanes : (j + 1) * lanes]
            full = jnp.where(mask, jnp.concatenate([part] * heads, axis=0), 0.0).astype(BF16)
            t = dot(
                qs[:, i * lanes : i * lanes + half_rows], full, (((1,), (0,)), ((), ()))
            )
            num = t if num is None else num + t
        nums.append(num)
    den = nums[0][:, lanes - 128 : lanes]
    at = half_rows - (lanes - 128)
    lane = lax.broadcasted_iota(jnp.int32, den.shape, 1)
    live = (lane >= at) & (lane < at + heads)
    inv = jnp.where(live, 1.0 / (jnp.where(live, den, 1.0) + EPSILON), 0.0)
    high = inv.astype(BF16)
    low = (inv - high.astype(F32)).astype(BF16)
    erow = lax.broadcasted_iota(jnp.int32, (128, lanes), 0) - at
    ecol = lax.broadcasted_iota(jnp.int32, (128, lanes), 1)
    spread = jnp.where((ecol < half_rows) & (erow == ecol // sub), 1.0, 0.0).astype(BF16)
    nn = (((1,), (0,)), ((), ()))
    scale = dot(high, spread, nn) + dot(low, spread, nn)
    for j in range(2):
        a = (nums[j] * scale).astype(BF16)
        att[:, j * half_rows : (j + 1) * half_rows] = a[:, 0:half_rows]

    for k in range(1, PLANES):
        which = (y_own + 4 * k) % (4 * PLANES)
        wait_block(which)
        send_block(which, core_peer, 12 + k)
    for zz in range(PLANES):
        for yy in range(2):
            wait_block(4 * zz + 2 * yy + 1 - core)

    per = block * wog.shape[0] // TILES
    step = per // 256
    blocks = wog.shape[0] // TILES

    def tile(t):
        return jnp.concatenate([wog[t * blocks + b] for b in range(blocks)], axis=0)

    p_copies = []
    for t in range(TILES):
        span = pl.ds(t * per, per)
        po[:, t * per : (t + 1) * per] = dot(att[rows : 2 * rows, :], tile(t), NT).astype(BF16)
        c = remote(po.at[:, span], pin.at[:, span], p_send.at[t], p_recv.at[t], x_peer)
        c.start()
        p_copies.append(c)
    for t in range(TILES):
        acc[:, t * per : (t + 1) * per] = dot(att[0:rows, :], tile(t), NT)
    for t in range(TILES):
        p_copies[t].wait_recv()
        a = acc[:, t * per : (t + 1) * per] + pin[:, t * per : (t + 1) * per].astype(F32)
        out_ref[:, t * per : (t + 1) * per] = a.astype(BF16)

    for c in x_copies + w_copies + [c_core, c_y, c_p] + p_copies:
        c.wait_send()
    for k in range(1, PLANES):
        @pl.when(z + k < PLANES)
        def _():
            remote(zb, zst.at[k - 1], s_send.at[1 + k], s_recv.at[1 + k], z_peer(k)).wait_send()


CHUNK = 80
TILES = 2


def fused(frames_x, qkv_weight, out_weight):
    _, row_count, col_count, d = frames_x.shape
    rows = row_count * col_count
    half_rows = qkv_weight.shape[1]
    width, cols = out_weight.shape
    frames = 4 * PLANES
    block = -(-cols // 16) * 16
    wide = -(-d // 256) * 256
    lanes = 512
    any_space = pl.BlockSpec(memory_space=pl.ANY)
    dma = pltpu.SemaphoreType.DMA
    v = pltpu.VMEM
    out = pl.pallas_call(
        kernel,
        out_shape=jax.ShapeDtypeStruct((rows, frames * block), BF16),
        in_specs=[any_space] * 3,
        out_specs=pl.BlockSpec(memory_space=pltpu.VMEM),
        scratch_shapes=[
            v((rows, d), BF16), v((rows, d), BF16), v((2 * rows, wide), BF16), v((2 * rows, wide), BF16),
            v(qkv_weight.shape, BF16), v((width, cols), BF16), v((frames, block, width), BF16),
            v((2 * rows, 2 * lanes), BF16), v((2 * rows, 2 * lanes), BF16), v((2 * rows, 2 * lanes), BF16),
            v((HD, 2 * lanes), F32), v((HD, 2 * lanes), BF16), v((HD, 2 * lanes), BF16),
            v((HD, lanes), BF16), v((HD, lanes), BF16), v((HD, lanes), BF16),
            v((PLANES - 1, HD, lanes), BF16), v((HD, lanes), BF16), v((HD, lanes), BF16),
            v((HD, 2 * lanes), F32),
            v((2 * rows, width), BF16), v((rows, frames * block), BF16), v((rows, frames * block), BF16),
            v((rows, frames * block), F32),
            dma((5,)), dma((rows // CHUNK,)), dma((rows // CHUNK,)), dma((16,)), dma((frames,)),
            dma((2 + PLANES,)), dma((2 + PLANES,)), dma((TILES,)), dma((TILES,)),
        ],
        compiler_params=pltpu.CompilerParams(
            collective_id=0, has_side_effects=True, vmem_limit_bytes=56 * 2**20
        ),
    )(frames_x.reshape(rows, d), qkv_weight, out_weight)
    out = out.reshape(rows, frames, block)[:, :, :cols]
    return out.reshape(1, row_count, col_count, d)


def solution(mesh):
    in_specs = (P("frames", "heads", None, None), P(None, "heads", None), P("heads", "frames"))
    out_specs = P("frames", "heads", None, None)
    small = mesh.shape["frames"] == 4 * PLANES and mesh.shape["heads"] == 2
    return jax.shard_map(
        fused if small else on_device, mesh=mesh, in_specs=in_specs, out_specs=out_specs, check_vma=False
    )
```

```python
import functools

import jax
import jax.numpy as jnp
from jax import lax
from jax.experimental import pallas as pl
from jax.experimental.pallas import tpu as pltpu
from jax.sharding import PartitionSpec as P

HD = 112


EPSILON = 1e-06


def carried_in(part, axis, combine, identity):
    place = lax.axis_index(axis)
    gathered = jax.tree.map(lambda a: lax.all_gather(a, axis), part)
    state = jax.tree.map(lambda a, e: jnp.zeros_like(a) + jnp.asarray(e, a.dtype), part, identity)

    def one(turn, state):
        return combine(
            state, jax.tree.map(lambda a: lax.dynamic_index_in_dim(a, turn, 0, False), gathered)
        )

    return lax.fori_loop(0, place, one, state)


def add_states(earlier, later):
    return (earlier[0] + later[0], earlier[1] + later[1])


def on_device(frames_x, qkv_weight, out_weight):
    feature_count = qkv_weight.shape[2] // 2
    local_width = qkv_weight.shape[1] * 2
    head_count = local_width // HD
    highest = lax.Precision.HIGHEST
    weights = qkv_weight.reshape(3, local_width, feature_count)
    mixed = jnp.einsum(
        "frcd,sed->sfrce",
        lax.all_gather(frames_x, "heads", axis=1, tiled=True),
        weights,
        preferred_element_type=jnp.float32,
    )
    projected = jnp.stack([jax.nn.relu(mixed[0]), jax.nn.relu(mixed[1]), mixed[2]]).astype(
        jnp.bfloat16
    )
    frame_count, row_count, col_count = (projected.shape[1], projected.shape[2], projected.shape[3])
    tokens = frame_count * row_count * col_count
    query = projected[0].reshape(tokens, head_count, HD)
    keys = projected[1].reshape(tokens, head_count, HD)
    values = projected[2].reshape(tokens, head_count, HD)
    own_state = jnp.einsum("mhi,mhj->hij", keys, values, preferred_element_type=jnp.float32)
    own_total = jnp.sum(keys.astype(jnp.float32), axis=0)
    identity = (jnp.zeros_like(own_state), jnp.zeros_like(own_total))
    prior_state, prior_total = carried_in((own_state, own_total), "frames", add_states, identity)
    query_wide = query.astype(jnp.float32)
    numerator = jnp.einsum("mhi,hij->mhj", query_wide, prior_state + own_state, precision=highest)
    denominator = (
        jnp.einsum("mhi,hi->mh", query_wide, prior_total + own_total, precision=highest) + EPSILON
    )
    attended = (numerator / denominator[..., None]).astype(jnp.bfloat16)
    attended = attended.reshape(frame_count, row_count, col_count, local_width)
    by_rows = lax.all_to_all(attended, "heads", split_axis=1, concat_axis=3, tiled=True)
    full_rows = lax.all_gather(out_weight, "heads", axis=0, tiled=True)
    result = jnp.einsum(
        "frce,ed->frcd",
        by_rows,
        lax.all_gather(full_rows, "frames", axis=1, tiled=True),
        preferred_element_type=jnp.float32,
    )
    return result.astype(jnp.bfloat16)


MESH = pl.DeviceIdType.MESH
NT = (((1,), (1,)), ((), ()))
TN = (((0,), (0,)), ((), ()))
NN = (((1,), (0,)), ((), ()))
F32 = jnp.float32
BF16 = jnp.bfloat16
PLANES = 4


def dot(a, b, dims):
    return lax.dot_general(a, b, dims, preferred_element_type=F32)


def kernel(
    x_ref, w_ref, wo_ref, out_ref,
    xv, xp, xe, xo, wv, wov, wog, qs, ks, vs, st, stb, cst, yb, yst, zb, zst, pb, pst, cum,
    att, po, pin, acc,
    lsem, x_send, x_recv, w_send, w_recv, s_send, s_recv, p_send, p_recv,
):
    frame = lax.axis_index("frames")
    side = lax.axis_index("heads")
    core = frame % 2
    y = (frame // 2) % 2
    z = frame // 4
    rows, d = x_ref.shape
    half_rows = w_ref.shape[1]
    cols, width = wo_ref.shape
    block = wog.shape[1]
    wide = xe.shape[1]
    heads = width // HD
    sub = HD // 2
    pad = wide - d
    lanes = st.shape[1] // 2

    x_peer = (frame, 1 - side)
    core_peer = (frame + 1 - 2 * core, side)
    y_peer = (frame + 2 - 4 * y, side)

    def z_peer(step):
        return ((frame + 4 * step) % (4 * PLANES), side)

    peers = [x_peer, core_peer, y_peer] + [z_peer(k) for k in range(1, PLANES)]

    load_wo = pltpu.make_async_copy(wo_ref, wov, lsem.at[0])
    load_x = pltpu.make_async_copy(x_ref, xv, lsem.at[1])
    load_w = [pltpu.make_async_copy(w_ref.at[s], wv.at[s], lsem.at[2 + s]) for s in range(3)]

    barrier = pltpu.get_barrier_semaphore()
    for peer in peers:
        pl.semaphore_signal(barrier, inc=1, device_id=peer, device_id_type=MESH)
    load_wo.start()
    load_x.start()
    for s in (1, 2, 0):
        load_w[s].start()
    pl.semaphore_wait(barrier, len(peers))

    def remote(src, dst, send, recv, peer):
        return pltpu.make_async_remote_copy(
            src_ref=src, dst_ref=dst, send_sem=send, recv_sem=recv,
            device_id=peer, device_id_type=MESH,
        )

    parts = xp.shape[0] // CHUNK
    x_copies = []
    for k in range(parts):
        span = pl.ds(k * CHUNK, CHUNK)
        c = remote(x_ref.at[span], xp.at[span], x_send.at[k], x_recv.at[k], x_peer)
        c.start()
        x_copies.append(c)

    load_wo.wait()
    row = lax.broadcasted_iota(jnp.int32, (width, width), 0)
    col = lax.broadcasted_iota(jnp.int32, (width, width), 1)
    target = jnp.where(col < half_rows, 2 * col, 2 * (col - half_rows) + 1)
    order = jnp.where(row == target, 1.0, 0.0).astype(BF16)
    wog[frame, pl.ds(0, cols), :] = dot(wov[...], order, NN).astype(BF16)

    wog[frame, pl.ds(cols, block - cols), :] = jnp.zeros((block - cols, width), BF16)
    w_copies = []

    def send_block(which, peer, slot):
        c = remote(wog.at[which], wog.at[which], w_send.at[slot], w_recv.at[which], peer)
        c.start()
        w_copies.append(c)

    def wait_block(which):
        remote(wog.at[which], wog.at[which], w_send.at[0], w_recv.at[which], core_peer).wait_recv()

    for k in range(1, PLANES):
        send_block(frame, z_peer(k), k - 1)
    send_block(frame, y_peer, 3)
    send_block(frame, core_peer, 4)

    def place(src, at, count, start):
        xe[start : start + count, 0:d] = src[at : at + count, :]
        xe[start : start + count, d:wide] = jnp.zeros((count, pad), BF16)
        xo[start : start + count, pad:wide] = src[at : at + count, :]
        xo[start : start + count, 0:pad] = jnp.zeros((count, pad), BF16)

    def project(s, dst, start, count, relu):
        for j, (src, lo) in enumerate(((xe, 0), (xo, d - pad))):
            p = dot(src[start : start + count, :], wv[s, :, lo : lo + wide], NT)
            if relu:
                p = jnp.maximum(p, 0.0)
            dst[start : start + count, j * lanes : j * lanes + half_rows] = p.astype(BF16)

    total = qs.shape[0]
    vs[:, half_rows:lanes] = jnp.ones((total, lanes - half_rows), BF16)
    vs[:, lanes + half_rows : 2 * lanes] = jnp.zeros((total, lanes - half_rows), BF16)

    load_x.wait()
    place(xv, 0, rows, 0)
    load_w[1].wait()
    project(1, ks, 0, rows, True)
    load_w[2].wait()
    project(2, vs, 0, rows, False)

    y_own = 4 * z + 2 * (1 - y) + core

    def forward_z(k):
        which = (frame + 4 * (PLANES - k)) % (4 * PLANES)
        wait_block(which)
        send_block(which, y_peer, 5 + 2 * k)
        send_block(which, core_peer, 6 + 2 * k)

    wait_block(y_own)
    send_block(y_own, core_peer, 5)

    load_w[0].wait()
    project(0, qs, 0, rows, True)

    for k in range(parts):
        x_copies[k].wait_recv()
        place(xp, k * CHUNK, CHUNK, rows + k * CHUNK)
        project(1, ks, rows + k * CHUNK, CHUNK, True)
        project(2, vs, rows + k * CHUNK, CHUNK, False)

    srow = lax.broadcasted_iota(jnp.int32, (half_rows, lanes), 0) // sub
    scol = lax.broadcasted_iota(jnp.int32, (half_rows, lanes), 1)
    mask = srow == jnp.where(scol < half_rows, scol // sub, scol - half_rows)

    for i in range(2):
        for j in range(2):
            full = dot(
                ks[:, i * lanes : i * lanes + half_rows],
                vs[:, j * lanes : (j + 1) * lanes],
                TN,
            )
            full = jnp.where(mask, full, 0.0)
            small = full[0:sub]
            for h in range(1, heads):
                small = small + full[h * sub : (h + 1) * sub]
            st[i * sub : (i + 1) * sub, j * lanes : (j + 1) * lanes] = small
    stb[...] = st[...].astype(BF16)
    c_core = remote(stb, cst, s_send.at[0], s_recv.at[0], core_peer)
    c_core.start()
    c_core.wait_recv()

    mine = pl.ds(pl.multiple_of(core * lanes, 128), lanes)
    other = pl.ds(pl.multiple_of((1 - core) * lanes, 128), lanes)
    pair = st[:, mine] + cst[:, mine].astype(F32)
    yb[...] = pair.astype(BF16)
    c_y = remote(yb, yst, s_send.at[1], s_recv.at[1], y_peer)
    c_y.start()
    c_y.wait_recv()
    zb[...] = (pair + yst[...].astype(F32)).astype(BF16)

    for k in range(1, PLANES):
        @pl.when(z + k < PLANES)
        def _():
            remote(zb, zst.at[k - 1], s_send.at[1 + k], s_recv.at[1 + k], z_peer(k)).start()

    for k in range(1, PLANES):
        forward_z(k)

    project(0, qs, rows, rows, True)

    cum[...] = st[...] + cst[...].astype(F32) * core.astype(F32)
    prior = yst[...].astype(F32) * y.astype(F32)
    pb[...] = prior.astype(BF16)
    acc[0:HD, 0:lanes] = prior
    for k in range(1, PLANES):
        @pl.when(z >= k)
        def _():
            remote(zb, zst.at[k - 1], s_send.at[1 + k], s_recv.at[1 + k], z_peer(k)).wait_recv()
            acc[0:HD, 0:lanes] += zst[k - 1].astype(F32)
    pb[...] = acc[0:HD, 0:lanes].astype(BF16)
    c_p = remote(pb, pst, s_send.at[1 + PLANES], s_recv.at[1 + PLANES], core_peer)
    c_p.start()
    cum[:, mine] += acc[0:HD, 0:lanes]
    c_p.wait_recv()
    cum[:, other] += pst[...].astype(F32)

    nums = []
    for j in range(2):
        num = None
        for i in range(2):
            part = cum[i * sub : (i + 1) * sub, j * lanes : (j + 1) * lanes]
            full = jnp.where(mask, jnp.concatenate([part] * heads, axis=0), 0.0).astype(BF16)
            t = dot(
                qs[:, i * lanes : i * lanes + half_rows], full, NN
            )
            num = t if num is None else num + t
        nums.append(num)
    den = nums[0][:, lanes - 128 : lanes]
    at = half_rows - (lanes - 128)
    lane = lax.broadcasted_iota(jnp.int32, den.shape, 1)
    live = (lane >= at) & (lane < at + heads)
    inv = jnp.where(live, 1.0 / (jnp.where(live, den, 1.0) + EPSILON), 0.0)
    high = inv.astype(BF16)
    low = (inv - high.astype(F32)).astype(BF16)
    erow = lax.broadcasted_iota(jnp.int32, (128, lanes), 0) - at
    ecol = lax.broadcasted_iota(jnp.int32, (128, lanes), 1)
    spread = jnp.where((ecol < half_rows) & (erow == ecol // sub), 1.0, 0.0).astype(BF16)
    scale = dot(high, spread, NN) + dot(low, spread, NN)
    for j in range(2):
        a = (nums[j] * scale).astype(BF16)
        att[:, j * half_rows : (j + 1) * half_rows] = a[:, 0:half_rows]

    for k in range(1, PLANES):
        which = (y_own + 4 * k) % (4 * PLANES)
        wait_block(which)
        send_block(which, core_peer, 12 + k)
    for zz in range(PLANES):
        for yy in range(2):
            wait_block(4 * zz + 2 * yy + 1 - core)

    per = block * wog.shape[0] // TILES
    blocks = wog.shape[0] // TILES

    def tile(t):
        return jnp.concatenate([wog[t * blocks + b] for b in range(blocks)], axis=0)

    p_copies = []
    for t in range(TILES):
        span = pl.ds(t * per, per)
        po[:, t * per : (t + 1) * per] = dot(att[rows : 2 * rows, :], tile(t), NT).astype(BF16)
        c = remote(po.at[:, span], pin.at[:, span], p_send.at[t], p_recv.at[t], x_peer)
        c.start()
        p_copies.append(c)
    for t in range(TILES):
        acc[:, t * per : (t + 1) * per] = dot(att[0:rows, :], tile(t), NT)
    for t in range(TILES):
        p_copies[t].wait_recv()
        a = acc[:, t * per : (t + 1) * per] + pin[:, t * per : (t + 1) * per].astype(F32)
        for b in range(blocks):
            f = t * blocks + b
            out_ref[:, f * cols : (f + 1) * cols] = a[:, b * block : b * block + cols].astype(BF16)

    for c in x_copies + w_copies + [c_core, c_y, c_p] + p_copies:
        c.wait_send()
    for k in range(1, PLANES):
        @pl.when(z + k < PLANES)
        def _():
            remote(zb, zst.at[k - 1], s_send.at[1 + k], s_recv.at[1 + k], z_peer(k)).wait_send()


CHUNK = 80
TILES = 2


def fused(frames_x, qkv_weight, out_weight):
    _, row_count, col_count, d = frames_x.shape
    rows = row_count * col_count
    half_rows = qkv_weight.shape[1]
    width, cols = out_weight.shape
    frames = 4 * PLANES
    block = -(-cols // 16) * 16
    wide = -(-d // 256) * 256
    lanes = 512
    any_space = pl.BlockSpec(memory_space=pl.ANY)
    dma = pltpu.SemaphoreType.DMA
    v = pltpu.VMEM
    out = pl.pallas_call(
        kernel,
        out_shape=jax.ShapeDtypeStruct((rows, d), BF16),
        in_specs=[any_space] * 3,
        out_specs=pl.BlockSpec(memory_space=pltpu.VMEM),
        scratch_shapes=[
            v((rows, d), BF16), v((rows, d), BF16), v((2 * rows, wide), BF16), v((2 * rows, wide), BF16),
            v(qkv_weight.shape, BF16), v((cols, width), BF16), v((frames, block, width), BF16),
            v((2 * rows, 2 * lanes), BF16), v((2 * rows, 2 * lanes), BF16), v((2 * rows, 2 * lanes), BF16),
            v((HD, 2 * lanes), F32), v((HD, 2 * lanes), BF16), v((HD, 2 * lanes), BF16),
            v((HD, lanes), BF16), v((HD, lanes), BF16), v((HD, lanes), BF16),
            v((PLANES - 1, HD, lanes), BF16), v((HD, lanes), BF16), v((HD, lanes), BF16),
            v((HD, 2 * lanes), F32),
            v((2 * rows, width), BF16), v((rows, frames * block), BF16), v((rows, frames * block), BF16),
            v((rows, frames * block), F32),
            dma((5,)), dma((rows // CHUNK,)), dma((rows // CHUNK,)), dma((16,)), dma((frames,)),
            dma((2 + PLANES,)), dma((2 + PLANES,)), dma((TILES,)), dma((TILES,)),
        ],
        compiler_params=pltpu.CompilerParams(
            collective_id=0, has_side_effects=True, vmem_limit_bytes=56 * 2**20
        ),
    )(frames_x.reshape(rows, d), qkv_weight, out_weight.T)
    return out.reshape(1, row_count, col_count, d)


def solution(mesh):
    in_specs = (P("frames", "heads", None, None), P(None, "heads", None), P("heads", "frames"))
    out_specs = P("frames", "heads", None, None)
    small = mesh.shape["frames"] == 4 * PLANES and mesh.shape["heads"] == 2
    return jax.shard_map(
        fused if small else on_device, mesh=mesh, in_specs=in_specs, out_specs=out_specs, check_vma=False
    )
```

```python
import functools

import jax
import jax.numpy as jnp
from jax import lax
from jax.experimental import pallas as pl
from jax.experimental.pallas import tpu as pltpu
from jax.sharding import PartitionSpec as P

HD = 112


EPSILON = 1e-06


def carried_in(part, axis, combine, identity):
    place = lax.axis_index(axis)
    gathered = jax.tree.map(lambda a: lax.all_gather(a, axis), part)
    state = jax.tree.map(lambda a, e: jnp.zeros_like(a) + jnp.asarray(e, a.dtype), part, identity)

    def one(turn, state):
        return combine(
            state, jax.tree.map(lambda a: lax.dynamic_index_in_dim(a, turn, 0, False), gathered)
        )

    return lax.fori_loop(0, place, one, state)


def add_states(earlier, later):
    return (earlier[0] + later[0], earlier[1] + later[1])


def on_device(frames_x, qkv_weight, out_weight):
    feature_count = qkv_weight.shape[2] // 2
    local_width = qkv_weight.shape[1] * 2
    head_count = local_width // HD
    highest = lax.Precision.HIGHEST
    weights = qkv_weight.reshape(3, local_width, feature_count)
    mixed = jnp.einsum(
        "frcd,sed->sfrce",
        lax.all_gather(frames_x, "heads", axis=1, tiled=True),
        weights,
        preferred_element_type=jnp.float32,
    )
    projected = jnp.stack([jax.nn.relu(mixed[0]), jax.nn.relu(mixed[1]), mixed[2]]).astype(
        jnp.bfloat16
    )
    frame_count, row_count, col_count = (projected.shape[1], projected.shape[2], projected.shape[3])
    tokens = frame_count * row_count * col_count
    query = projected[0].reshape(tokens, head_count, HD)
    keys = projected[1].reshape(tokens, head_count, HD)
    values = projected[2].reshape(tokens, head_count, HD)
    own_state = jnp.einsum("mhi,mhj->hij", keys, values, preferred_element_type=jnp.float32)
    own_total = jnp.sum(keys.astype(jnp.float32), axis=0)
    identity = (jnp.zeros_like(own_state), jnp.zeros_like(own_total))
    prior_state, prior_total = carried_in((own_state, own_total), "frames", add_states, identity)
    query_wide = query.astype(jnp.float32)
    numerator = jnp.einsum("mhi,hij->mhj", query_wide, prior_state + own_state, precision=highest)
    denominator = (
        jnp.einsum("mhi,hi->mh", query_wide, prior_total + own_total, precision=highest) + EPSILON
    )
    attended = (numerator / denominator[..., None]).astype(jnp.bfloat16)
    attended = attended.reshape(frame_count, row_count, col_count, local_width)
    by_rows = lax.all_to_all(attended, "heads", split_axis=1, concat_axis=3, tiled=True)
    full_rows = lax.all_gather(out_weight, "heads", axis=0, tiled=True)
    result = jnp.einsum(
        "frce,ed->frcd",
        by_rows,
        lax.all_gather(full_rows, "frames", axis=1, tiled=True),
        preferred_element_type=jnp.float32,
    )
    return result.astype(jnp.bfloat16)


MESH = pl.DeviceIdType.MESH
NT = (((1,), (1,)), ((), ()))
TN = (((0,), (0,)), ((), ()))
NN = (((1,), (0,)), ((), ()))
F32 = jnp.float32
BF16 = jnp.bfloat16
PLANES = 4


def dot(a, b, dims):
    return lax.dot_general(a, b, dims, preferred_element_type=F32)


def kernel(
    x_ref, w_ref, wo_ref, out_ref,
    xv, xp, xe, xo, wv, wov, wog, qs, ks, vs, st, stb, cst, yb, yst, zb, zst, pb, pst, cum,
    big, att, po, pin, acc,
    lsem, x_send, x_recv, w_send, w_recv, s_send, s_recv, p_send, p_recv,
):
    frame = lax.axis_index("frames")
    side = lax.axis_index("heads")
    core = frame % 2
    y = (frame // 2) % 2
    z = frame // 4
    rows, d = x_ref.shape
    half_rows = w_ref.shape[1]
    cols, width = wo_ref.shape
    block = wog.shape[0] // (4 * PLANES)
    wide = xe.shape[1]
    heads = width // HD
    sub = HD // 2
    pad = wide - d
    lanes = st.shape[1] // 2

    x_peer = (frame, 1 - side)
    core_peer = (frame + 1 - 2 * core, side)
    y_peer = (frame + 2 - 4 * y, side)

    def z_peer(step):
        return ((frame + 4 * step) % (4 * PLANES), side)

    peers = [x_peer, core_peer, y_peer] + [z_peer(k) for k in range(1, PLANES)]

    load_wo = pltpu.make_async_copy(wo_ref, wov, lsem.at[0])
    load_x = pltpu.make_async_copy(x_ref, xv, lsem.at[1])
    load_w = [pltpu.make_async_copy(w_ref.at[s], wv.at[s], lsem.at[2 + s]) for s in range(3)]

    barrier = pltpu.get_barrier_semaphore()
    for peer in peers:
        pl.semaphore_signal(barrier, inc=1, device_id=peer, device_id_type=MESH)
    load_wo.start()
    load_x.start()
    for s in (1, 2, 0):
        load_w[s].start()
    pl.semaphore_wait(barrier, len(peers))

    def remote(src, dst, send, recv, peer):
        return pltpu.make_async_remote_copy(
            src_ref=src, dst_ref=dst, send_sem=send, recv_sem=recv,
            device_id=peer, device_id_type=MESH,
        )

    parts = xp.shape[0] // CHUNK
    x_copies = []
    for k in range(parts):
        span = pl.ds(k * CHUNK, CHUNK)
        c = remote(x_ref.at[span], xp.at[span], x_send.at[k], x_recv.at[k], x_peer)
        c.start()
        x_copies.append(c)

    load_wo.wait()
    row = lax.broadcasted_iota(jnp.int32, (width, width), 0)
    col = lax.broadcasted_iota(jnp.int32, (width, width), 1)
    target = jnp.where(col < half_rows, 2 * col, 2 * (col - half_rows) + 1)
    order = jnp.where(row == target, 1.0, 0.0).astype(BF16)
    own = dot(wov[...], order, NN).astype(BF16)
    wog[pl.ds(pl.multiple_of(frame * block, 16), block), :] = jnp.concatenate(
        [own, jnp.zeros((block - cols, width), BF16)], axis=0
    )
    sent = []

    def rows_of(which):
        return wog.at[pl.ds(pl.multiple_of(which * block, 16), block)]

    def send_block(which, peer, slot, *conds):
        c = remote(rows_of(which), rows_of(which), w_send.at[slot], w_recv.at[which], peer)
        under(conds, c.start)
        sent.append((conds, c))

    def under(conds, act):
        if not conds:
            act()
            return
        cond = conds[0]
        for extra in conds[1:]:
            cond = cond & extra
        pl.when(cond)(act)

    def wait_block(which, *conds):
        c = remote(rows_of(which), rows_of(which), w_send.at[0], w_recv.at[which], core_peer)
        under(conds, c.wait_recv)

    down, up = z_peer(PLANES - 1), z_peer(1)
    has_down, has_up = z > 0, z < PLANES - 1
    send_block(frame, down, 0, has_down)
    send_block(frame, up, 1, has_up)
    send_block(frame, y_peer, 2)
    send_block(frame, core_peer, 3)

    def pass_on(k):
        below = (frame + 4 * (PLANES - k)) % (4 * PLANES)
        above = (frame + 4 * k) % (4 * PLANES)
        for j, (which, there, onward, more) in enumerate(
            ((below, z >= k, up, has_up), (above, z + k < PLANES, down, has_down))
        ):
            slot = 4 + 6 * (k - 1) + 3 * j
            wait_block(which, there)
            if k < PLANES - 1:
                send_block(which, onward, slot, there, more)
            send_block(which, y_peer, slot + 1, there)
            send_block(which, core_peer, slot + 2, there)

    def place(src, at, count, start):
        xe[start : start + count, 0:d] = src[at : at + count, :]
        xe[start : start + count, d:wide] = jnp.zeros((count, pad), BF16)
        xo[start : start + count, pad:wide] = src[at : at + count, :]
        xo[start : start + count, 0:pad] = jnp.zeros((count, pad), BF16)

    def project(s, dst, start, count, relu):
        for j, (src, lo) in enumerate(((xe, 0), (xo, d - pad))):
            p = dot(src[start : start + count, :], wv[s, :, lo : lo + wide], NT)
            if relu:
                p = jnp.maximum(p, 0.0)
            dst[start : start + count, j * lanes : j * lanes + half_rows] = p.astype(BF16)

    total = qs.shape[0]
    vs[:, half_rows:lanes] = jnp.ones((total, lanes - half_rows), BF16)
    vs[:, lanes + half_rows : 2 * lanes] = jnp.zeros((total, lanes - half_rows), BF16)

    load_x.wait()
    place(xv, 0, rows, 0)
    load_w[1].wait()
    project(1, ks, 0, rows, True)
    load_w[2].wait()
    project(2, vs, 0, rows, False)

    y_own = 4 * z + 2 * (1 - y) + core

    srow = lax.broadcasted_iota(jnp.int32, (half_rows, lanes), 0) // sub
    scol = lax.broadcasted_iota(jnp.int32, (half_rows, lanes), 1)
    mask = srow == jnp.where(scol < half_rows, scol // sub, scol - half_rows)

    def add_state(start, count, first):
        for i in range(2):
            for j in range(2):
                full = dot(
                    ks[start : start + count, i * lanes : i * lanes + half_rows],
                    vs[start : start + count, j * lanes : (j + 1) * lanes],
                    TN,
                )
                full = jnp.where(mask, full, 0.0)
                small = full[0:sub]
                for h in range(1, heads):
                    small = small + full[h * sub : (h + 1) * sub]
                at = (slice(i * sub, (i + 1) * sub), slice(j * lanes, (j + 1) * lanes))
                st[at] = small if first else st[at] + small

    add_state(0, rows, True)
    pass_on(1)
    wait_block(y_own)
    send_block(y_own, core_peer, 22)
    load_w[0].wait()
    for k in range(parts):
        x_copies[k].wait_recv()
        place(xp, k * CHUNK, CHUNK, rows + k * CHUNK)
        project(1, ks, rows + k * CHUNK, CHUNK, True)
        project(2, vs, rows + k * CHUNK, CHUNK, False)
        add_state(rows + k * CHUNK, CHUNK, False)
        if k == 0:
            pass_on(2)
    stb[...] = st[...].astype(BF16)
    c_core = remote(stb, cst, s_send.at[0], s_recv.at[0], core_peer)
    c_core.start()
    c_core.wait_recv()

    mine = pl.ds(pl.multiple_of(core * lanes, 128), lanes)
    other = pl.ds(pl.multiple_of((1 - core) * lanes, 128), lanes)
    pair = st[:, mine] + cst[:, mine].astype(F32)
    yb[...] = pair.astype(BF16)
    c_y = remote(yb, yst, s_send.at[1], s_recv.at[1], y_peer)
    c_y.start()
    c_y.wait_recv()
    zb[...] = (pair + yst[...].astype(F32)).astype(BF16)

    for k in range(1, PLANES):
        @pl.when(z + k < PLANES)
        def _():
            remote(zb, zst.at[k - 1], s_send.at[1 + k], s_recv.at[1 + k], z_peer(k)).start()

    pass_on(3)
    project(0, qs, 0, 2 * rows, True)

    cum[...] = st[...] + cst[...].astype(F32) * core.astype(F32)
    prior = yst[...].astype(F32) * y.astype(F32)
    pb[...] = prior.astype(BF16)
    acc[0:HD, 0:lanes] = prior
    for k in range(1, PLANES):
        @pl.when(z >= k)
        def _():
            remote(zb, zst.at[k - 1], s_send.at[1 + k], s_recv.at[1 + k], z_peer(k)).wait_recv()
            acc[0:HD, 0:lanes] += zst[k - 1].astype(F32)
    pb[...] = acc[0:HD, 0:lanes].astype(BF16)
    c_p = remote(pb, pst, s_send.at[1 + PLANES], s_recv.at[1 + PLANES], core_peer)
    c_p.start()
    cum[:, mine] += acc[0:HD, 0:lanes]
    c_p.wait_recv()
    cum[:, other] += pst[...].astype(F32)

    at = half_rows - (lanes - 128)
    erow = lax.broadcasted_iota(jnp.int32, (128, lanes), 0) - at
    ecol = lax.broadcasted_iota(jnp.int32, (128, lanes), 1)
    spread = jnp.where((ecol < half_rows) & (erow == ecol // sub), 1.0, 0.0).astype(BF16)
    for i in range(2):
        for j in range(2):
            part = cum[i * sub : (i + 1) * sub, j * lanes : (j + 1) * lanes]
            full = jnp.where(mask, jnp.concatenate([part] * heads, axis=0), 0.0).astype(BF16)
            big[i, j] = full

    def attend(start):
        nums = []
        for j in range(2):
            num = None
            for i in range(2):
                t = dot(qs[start : start + rows, i * lanes : i * lanes + half_rows], big[i, j], NN)
                num = t if num is None else num + t
            nums.append(num)
        den = nums[0][:, lanes - 128 : lanes]
        lane = lax.broadcasted_iota(jnp.int32, den.shape, 1)
        live = (lane >= at) & (lane < at + heads)
        inv = jnp.where(live, 1.0 / (jnp.where(live, den, 1.0) + EPSILON), 0.0)
        high = inv.astype(BF16)
        low = (inv - high.astype(F32)).astype(BF16)
        scale = dot(high, spread, NN) + dot(low, spread, NN)
        for j in range(2):
            a = (nums[j] * scale).astype(BF16)
            att[start : start + rows, j * half_rows : (j + 1) * half_rows] = a[:, 0:half_rows]

    attend(rows)

    for k in range(1, PLANES):
        which = (y_own + 4 * k) % (4 * PLANES)
        wait_block(which)
        send_block(which, core_peer, 22 + k)
    for zz in range(PLANES):
        for yy in range(2):
            wait_block(4 * zz + 2 * yy + 1 - core)

    per = wog.shape[0] // TILES
    p_copies = []
    for t in range(TILES):
        span = slice(t * per, (t + 1) * per)
        po[:, span] = dot(att[rows : 2 * rows, :], wog[span, :], NT).astype(BF16)
        at_cols = pl.ds(t * per, per)
        c = remote(po.at[:, at_cols], pin.at[:, at_cols], p_send.at[t], p_recv.at[t], x_peer)
        c.start()
        p_copies.append(c)
    attend(0)
    for t in range(TILES):
        span = slice(t * per, (t + 1) * per)
        acc[:, span] = dot(att[0:rows, :], wog[span, :], NT)
    done = 0
    for t in range(TILES):
        span = slice(t * per, (t + 1) * per)
        p_copies[t].wait_recv()
        acc[:, span] += pin[:, span].astype(F32)
        while done < 4 * PLANES and (done + 1) * block <= (t + 1) * per:
            piece = acc[:, done * block : done * block + cols]
            out_ref[:, done * cols : (done + 1) * cols] = piece.astype(BF16)
            done += 1

    for c in x_copies + [c_core, c_y, c_p] + p_copies:
        c.wait_send()
    for conds, c in sent:
        under(conds, c.wait_send)
    for k in range(1, PLANES):
        @pl.when(z + k < PLANES)
        def _():
            remote(zb, zst.at[k - 1], s_send.at[1 + k], s_recv.at[1 + k], z_peer(k)).wait_send()


CHUNK = 80
TILES = 3


def fused(frames_x, qkv_weight, out_weight):
    _, row_count, col_count, d = frames_x.shape
    rows = row_count * col_count
    half_rows = qkv_weight.shape[1]
    width, cols = out_weight.shape
    frames = 4 * PLANES
    block = -(-cols // 16) * 16
    wide = -(-d // 256) * 256
    lanes = 512
    any_space = pl.BlockSpec(memory_space=pl.ANY)
    dma = pltpu.SemaphoreType.DMA
    v = pltpu.VMEM
    out = pl.pallas_call(
        kernel,
        out_shape=jax.ShapeDtypeStruct((rows, d), BF16),
        in_specs=[any_space] * 3,
        out_specs=pl.BlockSpec(memory_space=pltpu.VMEM),
        scratch_shapes=[
            v((rows, d), BF16), v((rows, d), BF16), v((2 * rows, wide), BF16), v((2 * rows, wide), BF16),
            v(qkv_weight.shape, BF16), v((cols, width), BF16), v((frames * block, width), BF16),
            v((2 * rows, 2 * lanes), BF16), v((2 * rows, 2 * lanes), BF16), v((2 * rows, 2 * lanes), BF16),
            v((HD, 2 * lanes), F32), v((HD, 2 * lanes), BF16), v((HD, 2 * lanes), BF16),
            v((HD, lanes), BF16), v((HD, lanes), BF16), v((HD, lanes), BF16),
            v((PLANES - 1, HD, lanes), BF16), v((HD, lanes), BF16), v((HD, lanes), BF16),
            v((HD, 2 * lanes), F32),
            v((2, 2, half_rows, lanes), BF16),
            v((2 * rows, width), BF16), v((rows, frames * block), BF16), v((rows, frames * block), BF16),
            v((rows, frames * block), F32),
            dma((5,)), dma((rows // CHUNK,)), dma((rows // CHUNK,)), dma((26,)), dma((frames,)),
            dma((2 + PLANES,)), dma((2 + PLANES,)), dma((TILES,)), dma((TILES,)),
        ],
        compiler_params=pltpu.CompilerParams(
            collective_id=0, has_side_effects=True, vmem_limit_bytes=56 * 2**20
        ),
    )(frames_x.reshape(rows, d), qkv_weight, out_weight.T)
    return out.reshape(1, row_count, col_count, d)


def solution(mesh):
    in_specs = (P("frames", "heads", None, None), P(None, "heads", None), P("heads", "frames"))
    out_specs = P("frames", "heads", None, None)
    small = mesh.shape["frames"] == 4 * PLANES and mesh.shape["heads"] == 2
    return jax.shard_map(
        fused if small else on_device, mesh=mesh, in_specs=in_specs, out_specs=out_specs, check_vma=False
    )
```

```python
import functools

import jax
import jax.numpy as jnp
from jax import lax
from jax.experimental import pallas as pl
from jax.experimental.pallas import tpu as pltpu
from jax.sharding import PartitionSpec as P

HD = 112


EPSILON = 1e-06


def carried_in(part, axis, combine, identity):
    place = lax.axis_index(axis)
    gathered = jax.tree.map(lambda a: lax.all_gather(a, axis), part)
    state = jax.tree.map(lambda a, e: jnp.zeros_like(a) + jnp.asarray(e, a.dtype), part, identity)

    def one(turn, state):
        return combine(
            state, jax.tree.map(lambda a: lax.dynamic_index_in_dim(a, turn, 0, False), gathered)
        )

    return lax.fori_loop(0, place, one, state)


def add_states(earlier, later):
    return (earlier[0] + later[0], earlier[1] + later[1])


def on_device(frames_x, qkv_weight, out_weight):
    feature_count = qkv_weight.shape[2] // 2
    local_width = qkv_weight.shape[1] * 2
    head_count = local_width // HD
    highest = lax.Precision.HIGHEST
    weights = qkv_weight.reshape(3, local_width, feature_count)
    mixed = jnp.einsum(
        "frcd,sed->sfrce",
        lax.all_gather(frames_x, "heads", axis=1, tiled=True),
        weights,
        preferred_element_type=jnp.float32,
    )
    projected = jnp.stack([jax.nn.relu(mixed[0]), jax.nn.relu(mixed[1]), mixed[2]]).astype(
        jnp.bfloat16
    )
    frame_count, row_count, col_count = (projected.shape[1], projected.shape[2], projected.shape[3])
    tokens = frame_count * row_count * col_count
    query = projected[0].reshape(tokens, head_count, HD)
    keys = projected[1].reshape(tokens, head_count, HD)
    values = projected[2].reshape(tokens, head_count, HD)
    own_state = jnp.einsum("mhi,mhj->hij", keys, values, preferred_element_type=jnp.float32)
    own_total = jnp.sum(keys.astype(jnp.float32), axis=0)
    identity = (jnp.zeros_like(own_state), jnp.zeros_like(own_total))
    prior_state, prior_total = carried_in((own_state, own_total), "frames", add_states, identity)
    query_wide = query.astype(jnp.float32)
    numerator = jnp.einsum("mhi,hij->mhj", query_wide, prior_state + own_state, precision=highest)
    denominator = (
        jnp.einsum("mhi,hi->mh", query_wide, prior_total + own_total, precision=highest) + EPSILON
    )
    attended = (numerator / denominator[..., None]).astype(jnp.bfloat16)
    attended = attended.reshape(frame_count, row_count, col_count, local_width)
    by_rows = lax.all_to_all(attended, "heads", split_axis=1, concat_axis=3, tiled=True)
    full_rows = lax.all_gather(out_weight, "heads", axis=0, tiled=True)
    result = jnp.einsum(
        "frce,ed->frcd",
        by_rows,
        lax.all_gather(full_rows, "frames", axis=1, tiled=True),
        preferred_element_type=jnp.float32,
    )
    return result.astype(jnp.bfloat16)


MESH = pl.DeviceIdType.MESH
NT = (((1,), (1,)), ((), ()))
TN = (((0,), (0,)), ((), ()))
NN = (((1,), (0,)), ((), ()))
F32 = jnp.float32
BF16 = jnp.bfloat16
PLANES = 4


def dot(a, b, dims):
    return lax.dot_general(a, b, dims, preferred_element_type=F32)


def kernel(
    x_ref, w_ref, wo_ref, out_ref,
    xv, xp, xe, xo, wv, wov, wog, qs, ks, vs, st, stb, cst, yb, yst, zb, zst, pb, pst, cum,
    big, att, po, pin, acc,
    lsem, x_send, x_recv, w_send, w_recv, s_send, s_recv, p_send, p_recv,
):
    frame = lax.axis_index("frames")
    side = lax.axis_index("heads")
    core = frame % 2
    y = (frame // 2) % 2
    z = frame // 4
    rows, d = x_ref.shape
    half_rows = w_ref.shape[1]
    cols, width = wo_ref.shape
    block = wog.shape[0] // (4 * PLANES)
    wide = xe.shape[1]
    heads = width // HD
    sub = HD // 2
    pad = wide - d
    lanes = st.shape[1] // 2

    x_peer = (frame, 1 - side)
    core_peer = (frame + 1 - 2 * core, side)
    y_peer = (frame + 2 - 4 * y, side)

    def z_peer(step):
        return ((frame + 4 * step) % (4 * PLANES), side)

    peers = [x_peer, core_peer, y_peer] + [z_peer(k) for k in range(1, PLANES)]

    load_wo = pltpu.make_async_copy(wo_ref, wov, lsem.at[0])
    load_x = pltpu.make_async_copy(x_ref, xv, lsem.at[1])
    load_w = [pltpu.make_async_copy(w_ref.at[s], wv.at[s], lsem.at[2 + s]) for s in range(3)]

    barrier = pltpu.get_barrier_semaphore()
    for peer in peers:
        pl.semaphore_signal(barrier, inc=1, device_id=peer, device_id_type=MESH)
    load_wo.start()
    load_x.start()
    for s in (1, 2, 0):
        load_w[s].start()
    pl.semaphore_wait(barrier, len(peers))

    def remote(src, dst, send, recv, peer):
        return pltpu.make_async_remote_copy(
            src_ref=src, dst_ref=dst, send_sem=send, recv_sem=recv,
            device_id=peer, device_id_type=MESH,
        )

    parts = xp.shape[0] // CHUNK
    x_copies = []
    for k in range(parts):
        span = pl.ds(k * CHUNK, CHUNK)
        c = remote(x_ref.at[span], xp.at[span], x_send.at[k], x_recv.at[k], x_peer)
        c.start()
        x_copies.append(c)

    load_wo.wait()
    row = lax.broadcasted_iota(jnp.int32, (width, width), 0)
    col = lax.broadcasted_iota(jnp.int32, (width, width), 1)
    target = jnp.where(col < half_rows, 2 * col, 2 * (col - half_rows) + 1)
    order = jnp.where(row == target, 1.0, 0.0).astype(BF16)
    own = dot(wov[...], order, NN).astype(BF16)
    wog[pl.ds(pl.multiple_of(frame * block, 16), block), :] = jnp.concatenate(
        [own, jnp.zeros((block - cols, width), BF16)], axis=0
    )
    sent = []

    def rows_of(which):
        return wog.at[pl.ds(pl.multiple_of(which * block, 16), block)]

    def send_block(which, peer, slot, *conds):
        c = remote(rows_of(which), rows_of(which), w_send.at[slot], w_recv.at[which], peer)
        under(conds, c.start)
        sent.append((conds, c))

    def under(conds, act):
        if not conds:
            act()
            return
        cond = conds[0]
        for extra in conds[1:]:
            cond = cond & extra
        pl.when(cond)(act)

    def wait_block(which, *conds):
        c = remote(rows_of(which), rows_of(which), w_send.at[0], w_recv.at[which], core_peer)
        under(conds, c.wait_recv)

    down, up = z_peer(PLANES - 1), z_peer(1)
    has_down, has_up = z > 0, z < PLANES - 1
    send_block(frame, down, 0, has_down)
    send_block(frame, up, 1, has_up)
    send_block(frame, y_peer, 2)
    send_block(frame, core_peer, 3)

    def pass_on(k):
        below = (frame + 4 * (PLANES - k)) % (4 * PLANES)
        above = (frame + 4 * k) % (4 * PLANES)
        for j, (which, there, onward, more) in enumerate(
            ((below, z >= k, up, has_up), (above, z + k < PLANES, down, has_down))
        ):
            slot = 4 + 6 * (k - 1) + 3 * j
            wait_block(which, there)
            if k < PLANES - 1:
                send_block(which, onward, slot, there, more)
            send_block(which, y_peer, slot + 1, there)
            send_block(which, core_peer, slot + 2, there)

    def place(src, at, count, start):
        xe[start : start + count, 0:d] = src[at : at + count, :]
        xe[start : start + count, d:wide] = jnp.zeros((count, pad), BF16)
        xo[start : start + count, pad:wide] = src[at : at + count, :]
        xo[start : start + count, 0:pad] = jnp.zeros((count, pad), BF16)

    def project(s, dst, start, count, relu):
        for j, (src, lo) in enumerate(((xe, 0), (xo, d - pad))):
            p = dot(src[start : start + count, :], wv[s, :, lo : lo + wide], NT)
            if relu:
                p = jnp.maximum(p, 0.0)
            dst[start : start + count, j * lanes : j * lanes + half_rows] = p.astype(BF16)

    total = qs.shape[0]
    vs[:, half_rows:lanes] = jnp.ones((total, lanes - half_rows), BF16)
    vs[:, lanes + half_rows : 2 * lanes] = jnp.zeros((total, lanes - half_rows), BF16)

    load_x.wait()
    place(xv, 0, rows, 0)
    load_w[1].wait()
    project(1, ks, 0, rows, True)
    pass_on(1)
    load_w[2].wait()
    project(2, vs, 0, rows, False)

    y_own = 4 * z + 2 * (1 - y) + core

    srow = lax.broadcasted_iota(jnp.int32, (half_rows, lanes), 0) // sub
    scol = lax.broadcasted_iota(jnp.int32, (half_rows, lanes), 1)
    mask = srow == jnp.where(scol < half_rows, scol // sub, scol - half_rows)

    def add_state(start, count, first):
        for i in range(2):
            for j in range(2):
                full = dot(
                    ks[start : start + count, i * lanes : i * lanes + half_rows],
                    vs[start : start + count, j * lanes : (j + 1) * lanes],
                    TN,
                )
                full = jnp.where(mask, full, 0.0)
                small = full[0:sub]
                for h in range(1, heads):
                    small = small + full[h * sub : (h + 1) * sub]
                at = (slice(i * sub, (i + 1) * sub), slice(j * lanes, (j + 1) * lanes))
                st[at] = small if first else st[at] + small

    add_state(0, rows, True)
    wait_block(y_own)
    send_block(y_own, core_peer, 22)
    load_w[0].wait()
    for k in range(parts):
        x_copies[k].wait_recv()
        place(xp, k * CHUNK, CHUNK, rows + k * CHUNK)
        project(1, ks, rows + k * CHUNK, CHUNK, True)
        project(2, vs, rows + k * CHUNK, CHUNK, False)
        add_state(rows + k * CHUNK, CHUNK, False)
    stb[...] = st[...].astype(BF16)
    c_core = remote(stb, cst, s_send.at[0], s_recv.at[0], core_peer)
    c_core.start()
    pass_on(2)
    c_core.wait_recv()

    mine = pl.ds(pl.multiple_of(core * lanes, 128), lanes)
    other = pl.ds(pl.multiple_of((1 - core) * lanes, 128), lanes)
    pair = st[:, mine] + cst[:, mine].astype(F32)
    yb[...] = pair.astype(BF16)
    c_y = remote(yb, yst, s_send.at[1], s_recv.at[1], y_peer)
    c_y.start()
    c_y.wait_recv()
    zb[...] = (pair + yst[...].astype(F32)).astype(BF16)

    for k in range(1, PLANES):
        @pl.when(z + k < PLANES)
        def _():
            remote(zb, zst.at[k - 1], s_send.at[1 + k], s_recv.at[1 + k], z_peer(k)).start()

    project(0, qs, 0, 2 * rows, True)
    pass_on(3)

    cum[...] = st[...] + cst[...].astype(F32) * core.astype(F32)
    prior = yst[...].astype(F32) * y.astype(F32)
    pb[...] = prior.astype(BF16)
    acc[0:HD, 0:lanes] = prior
    for k in range(1, PLANES):
        @pl.when(z >= k)
        def _():
            remote(zb, zst.at[k - 1], s_send.at[1 + k], s_recv.at[1 + k], z_peer(k)).wait_recv()
            acc[0:HD, 0:lanes] += zst[k - 1].astype(F32)
    pb[...] = acc[0:HD, 0:lanes].astype(BF16)
    c_p = remote(pb, pst, s_send.at[1 + PLANES], s_recv.at[1 + PLANES], core_peer)
    c_p.start()
    cum[:, mine] += acc[0:HD, 0:lanes]
    c_p.wait_recv()
    cum[:, other] += pst[...].astype(F32)

    at = half_rows - (lanes - 128)
    erow = lax.broadcasted_iota(jnp.int32, (128, lanes), 0) - at
    ecol = lax.broadcasted_iota(jnp.int32, (128, lanes), 1)
    spread = jnp.where((ecol < half_rows) & (erow == ecol // sub), 1.0, 0.0).astype(BF16)
    for i in range(2):
        for j in range(2):
            part = cum[i * sub : (i + 1) * sub, j * lanes : (j + 1) * lanes]
            full = jnp.where(mask, jnp.concatenate([part] * heads, axis=0), 0.0).astype(BF16)
            big[i, j] = full

    def attend(start):
        nums = []
        for j in range(2):
            num = None
            for i in range(2):
                t = dot(qs[start : start + rows, i * lanes : i * lanes + half_rows], big[i, j], NN)
                num = t if num is None else num + t
            nums.append(num)
        den = nums[0][:, lanes - 128 : lanes]
        lane = lax.broadcasted_iota(jnp.int32, den.shape, 1)
        live = (lane >= at) & (lane < at + heads)
        inv = jnp.where(live, 1.0 / (jnp.where(live, den, 1.0) + EPSILON), 0.0)
        high = inv.astype(BF16)
        low = (inv - high.astype(F32)).astype(BF16)
        scale = dot(high, spread, NN) + dot(low, spread, NN)
        for j in range(2):
            a = (nums[j] * scale).astype(BF16)
            att[start : start + rows, j * half_rows : (j + 1) * half_rows] = a[:, 0:half_rows]

    attend(rows)

    for k in range(1, PLANES):
        which = (y_own + 4 * k) % (4 * PLANES)
        wait_block(which)
        send_block(which, core_peer, 22 + k)
    for zz in range(PLANES):
        for yy in range(2):
            wait_block(4 * zz + 2 * yy + 1 - core)

    per = wog.shape[0] // TILES
    p_copies = []
    for t in range(TILES):
        span = slice(t * per, (t + 1) * per)
        po[:, span] = dot(att[rows : 2 * rows, :], wog[span, :], NT).astype(BF16)
        at_cols = pl.ds(t * per, per)
        c = remote(po.at[:, at_cols], pin.at[:, at_cols], p_send.at[t], p_recv.at[t], x_peer)
        c.start()
        p_copies.append(c)
    attend(0)
    for t in range(TILES):
        span = slice(t * per, (t + 1) * per)
        acc[:, span] = dot(att[0:rows, :], wog[span, :], NT)
    done = 0
    for t in range(TILES):
        span = slice(t * per, (t + 1) * per)
        p_copies[t].wait_recv()
        acc[:, span] += pin[:, span].astype(F32)
        while done < 4 * PLANES and (done + 1) * block <= (t + 1) * per:
            piece = acc[:, done * block : done * block + cols]
            out_ref[:, done * cols : (done + 1) * cols] = piece.astype(BF16)
            done += 1

    for c in x_copies + [c_core, c_y, c_p] + p_copies:
        c.wait_send()
    for conds, c in sent:
        under(conds, c.wait_send)
    for k in range(1, PLANES):
        @pl.when(z + k < PLANES)
        def _():
            remote(zb, zst.at[k - 1], s_send.at[1 + k], s_recv.at[1 + k], z_peer(k)).wait_send()


CHUNK = 80
TILES = 3


def fused(frames_x, qkv_weight, out_weight):
    _, row_count, col_count, d = frames_x.shape
    rows = row_count * col_count
    half_rows = qkv_weight.shape[1]
    width, cols = out_weight.shape
    frames = 4 * PLANES
    block = -(-cols // 16) * 16
    wide = -(-d // 256) * 256
    lanes = 512
    any_space = pl.BlockSpec(memory_space=pl.ANY)
    dma = pltpu.SemaphoreType.DMA
    v = pltpu.VMEM
    out = pl.pallas_call(
        kernel,
        out_shape=jax.ShapeDtypeStruct((rows, d), BF16),
        in_specs=[any_space] * 3,
        out_specs=pl.BlockSpec(memory_space=pltpu.VMEM),
        scratch_shapes=[
            v((rows, d), BF16), v((rows, d), BF16), v((2 * rows, wide), BF16), v((2 * rows, wide), BF16),
            v(qkv_weight.shape, BF16), v((cols, width), BF16), v((frames * block, width), BF16),
            v((2 * rows, 2 * lanes), BF16), v((2 * rows, 2 * lanes), BF16), v((2 * rows, 2 * lanes), BF16),
            v((HD, 2 * lanes), F32), v((HD, 2 * lanes), BF16), v((HD, 2 * lanes), BF16),
            v((HD, lanes), BF16), v((HD, lanes), BF16), v((HD, lanes), BF16),
            v((PLANES - 1, HD, lanes), BF16), v((HD, lanes), BF16), v((HD, lanes), BF16),
            v((HD, 2 * lanes), F32),
            v((2, 2, half_rows, lanes), BF16),
            v((2 * rows, width), BF16), v((rows, frames * block), BF16), v((rows, frames * block), BF16),
            v((rows, frames * block), F32),
            dma((5,)), dma((rows // CHUNK,)), dma((rows // CHUNK,)), dma((26,)), dma((frames,)),
            dma((2 + PLANES,)), dma((2 + PLANES,)), dma((TILES,)), dma((TILES,)),
        ],
        compiler_params=pltpu.CompilerParams(
            collective_id=0, has_side_effects=True, vmem_limit_bytes=56 * 2**20
        ),
    )(frames_x.reshape(rows, d), qkv_weight, out_weight.T)
    return out.reshape(1, row_count, col_count, d)


def solution(mesh):
    in_specs = (P("frames", "heads", None, None), P(None, "heads", None), P("heads", "frames"))
    out_specs = P("frames", "heads", None, None)
    small = mesh.shape["frames"] == 4 * PLANES and mesh.shape["heads"] == 2
    return jax.shard_map(
        fused if small else on_device, mesh=mesh, in_specs=in_specs, out_specs=out_specs, check_vma=False
    )
```
